32 devices in a mesh: groups: 2 (over y), row: 4 (over z), col: 4 (over x, core).
Axes of the slice: x: 2, y: 2, z: 4, core: 2. Of those that a mesh axis runs over, the one named last changes fastest.
Arguments:
- base_density: bfloat16 [8, 8, 9, 184, 184], P(('groups', 'row'), 'col'), parts along dimension 0, as said below
- tangent_density: bfloat16 [8, 8, 9, 184, 184], P(('groups', 'row'), 'col'), parts along dimension 0, as said below
- pattern: int32 [4, 8, 9, 8, 8], P('row', 'col'), may hold values from 0 to 1, as said below
Outputs:
- tangent_step: bfloat16 [8, 8, 9, 184, 184], P(('groups', 'row'), 'col'), parts along dimension 0
The draws below stay inside these ranges and needn't reach their ends.
There are 2 independent parts, one for each index of `groups`. The reference program is written for one: setup_inputs(seed, part) draws one part's arguments, and reference() takes and returns one part's arrays. A program takes and returns all parts, laid end to end along the dimension named above; an argument that names none is the same for every part. Nothing has to cross between parts.
Inputs may be any that keep to these rules, and one draw needn't show every extreme that they name: pattern is symmetric: pattern[x, y, o, z, z'] equals pattern[(x + sx) mod 4, (y + sy) mod 8, 8 - o, z', z]; the blocks on the diagonal (o = 4, z = z') are kept. base_density is a symmetric matrix in the layout of the steps. tangent_density is a symmetric matrix in the layout of the steps.
All inputs are finite; a program needn't handle non-finite values.
Results may differ from the reference program's by a relative error of at most 0.0068.
Values may be sent and summed in bfloat16 or wider, within the bound.
A program may use at most 128 MiB of HBM per device.

```python
import jax
import jax.numpy as jnp
from jax import lax

BLOCK = 23
GZ = 8
GX = 4
GY = 8
TILE = 184


def mirror(field):
    stacked = []
    for offset in range(9):
        shift_x = offset // 3 - 1
        shift_y = offset % 3 - 1
        mate = jnp.roll(field[:, :, 8 - offset], (-shift_x, -shift_y), axis=(0, 1))
        stacked.append(field[:, :, offset] + jnp.swapaxes(mate, -1, -2))
    return jnp.stack(stacked, axis=2)


def draw_base_density(key, part):
    key = jax.random.fold_in(key, 11)
    noise_key, diag_key = jax.random.split(key)
    shape = (GX, GY, 9, TILE, TILE)
    spread = 0.5 / (6.75 * TILE) ** 0.5
    field = jax.random.normal(noise_key, shape, jnp.float32) * spread
    field = mirror(field)
    diagonal = jax.random.uniform(diag_key, (GX, GY, TILE), jnp.float32, 0.3, 0.7)
    rows = lax.broadcasted_iota(jnp.int32, (TILE, TILE), 0)
    cols = lax.broadcasted_iota(jnp.int32, (TILE, TILE), 1)
    identity = (rows == cols).astype(jnp.float32)
    centre = field[:, :, 4] + diagonal[:, :, :, None] * identity
    field = field.at[:, :, 4].set(centre)
    return field.astype(jnp.bfloat16)


def draw_tangent_density(key, part):
    key = jax.random.fold_in(key, 13)
    shape = (GX, GY, 9, TILE, TILE)
    spread = 0.35
    field = jax.random.normal(key, shape, jnp.float32) * spread
    return mirror(field).astype(jnp.bfloat16)


def draw_pattern(key, part):
    key = jax.random.fold_in(key, 17)
    coins = jax.random.randint(key, (GX, GY, 9, GZ, GZ), 0, 4)
    paired = mirror(coins)
    kept = (paired % 4 != 0).astype(jnp.int32)
    rows = lax.broadcasted_iota(jnp.int32, (GZ, GZ), 0)
    cols = lax.broadcasted_iota(jnp.int32, (GZ, GZ), 1)
    centre = jnp.maximum(kept[:, :, 4], (rows == cols).astype(jnp.int32))
    return kept.at[:, :, 4].set(centre)


def setup_inputs(seed: int = 0, part: int = 0) -> dict:
    key_of = jax.random.split(jax.random.key(seed), 4)
    part_splits = jax.random.split(jax.random.fold_in(key_of[3], part), 4)
    return {
        "base_density": draw_base_density(jax.random.fold_in(jax.random.fold_in(key_of[3], part), 71), part),
        "tangent_density": draw_tangent_density(jax.random.fold_in(jax.random.fold_in(key_of[3], part), 71), part),
        "pattern": draw_pattern(jax.random.fold_in(key_of[3], 71), part),
    }


def expand(pattern):
    wide = jnp.repeat(jnp.repeat(pattern, BLOCK, axis=-2), BLOCK, axis=-1)
    return wide.astype(jnp.float32)


def shifts(offset):
    return offset // 3 - 1, offset % 3 - 1


def joined(first_off, second_off):
    first_x, first_y = shifts(first_off)
    second_x, second_y = shifts(second_off)
    total_x = first_x + second_x
    total_y = first_y + second_y
    if abs(total_x) > 1 or abs(total_y) > 1:
        return -1
    return (total_x + 1) * 3 + total_y + 1


def tile_product(left, right):
    left_wide = left.astype(jnp.float32)
    totals = [None] * 9
    for first_off in range(9):
        shift_x, shift_y = shifts(first_off)
        moved = jnp.roll(right, (-shift_x, -shift_y), axis=(0, 1)).astype(jnp.float32)
        for second_off in range(9):
            target = joined(first_off, second_off)
            if target < 0:
                continue
            term = jnp.einsum('xyab,xybc->xyac', left_wide[:, :, first_off], moved[:, :, second_off], precision=lax.Precision.HIGHEST, preferred_element_type=jnp.float32)
            totals[target] = term if totals[target] is None else totals[target] + term
    return jnp.stack(totals, axis=2)


def reference(base_density, tangent_density, pattern):
    block_mask = expand(pattern)
    base_kept = (base_density.astype(jnp.float32) * block_mask).astype(jnp.bfloat16)
    tangent_kept = (tangent_density.astype(jnp.float32) * block_mask).astype(jnp.bfloat16)
    first_term = block_mask * tile_product(base_kept, tangent_kept)
    second_term = block_mask * tile_product(tangent_kept, base_kept)
    first_round = first_term.astype(jnp.bfloat16)
    summed = (first_term + second_term).astype(jnp.bfloat16)
    third_term = block_mask * tile_product(base_kept, first_round)
    fourth_term = block_mask * tile_product(summed, base_kept)
    result = 3.0 * (first_term + second_term) - 2.0 * (third_term + fourth_term)
    return result.astype(jnp.bfloat16)
```

```python
import functools

import jax
import jax.numpy as jnp
from jax import lax
from jax.experimental import pallas as pl
from jax.experimental.pallas import tpu as pltpu
from jax.sharding import PartitionSpec as P

BLOCK = 23
MESH = pl.DeviceIdType.MESH
ORDER = (0, 1, 2, 6, 7, 8, 3, 5, 4)


def shifts(offset):
    return (offset // 3 - 1, offset % 3 - 1)


def sources(target):
    out = []
    for first in range(9):
        fx, fy = shifts(first)
        tx, ty = shifts(target)
        sx, sy = tx - fx, ty - fy
        if abs(sx) <= 1 and abs(sy) <= 1:
            out.append((first, (sx + 1) * 3 + sy + 1))
    return out


def halo_plan():
    plan = []
    for dr in (1, -1):
        plan.append((dr, 0, 0, 3, 3))
        plan.append((dr, 0, 1, 4, 2))
    for dr in (1, -1):
        plan.append((dr, 1, 1, 4, 1))
        plan.append((dr, -1, 0, 4, 1))
    for first, count in ((1, 2), (4, 1), (7, 2)):
        plan.append((0, 1, 1, first, count))
    for first, count in ((0, 2), (4, 1), (6, 2)):
        plan.append((0, -1, 0, first, count))
    return plan


def place(col, offset):
    sx, sy = shifts(offset)
    y = col + sy
    return sx, y // 2, y % 2


def is_local(col, offset):
    sx, dc, _ = place(col, offset)
    return sx == 0 and dc == 0


HALO = halo_plan()
REMOTE = [(c, o) for o in ORDER for c in range(2) if not is_local(c, o)]


def kernel(
    rows, cols, base, tangent, pattern, out,
    q, p, mask, r32, rb, rt, f, gt, g, s,
    h_send, h_recv, r_send, r_recv, g_send, g_recv,
):
    group = lax.axis_index("groups")
    row = lax.axis_index("row")
    col = lax.axis_index("col")
    tile = base.shape[-1]

    def device(dr, dc):
        return (group, lax.rem(row + dr + rows, rows), lax.rem(col + dc + cols, cols))

    barrier = pltpu.get_barrier_semaphore()
    around = [(a, b) for a in (-1, 0, 1) for b in (-1, 0, 1) if (a, b) != (0, 0)]
    for dr, dc in around:
        pl.semaphore_signal(barrier, inc=1, device_id=device(dr, dc), device_id_type=MESH)

    blocks = pattern.shape[-1]
    up_r = lax.broadcasted_iota(jnp.int32, (tile, blocks), 0)
    up_c = lax.broadcasted_iota(jnp.int32, (tile, blocks), 1) * BLOCK
    up = ((up_r >= up_c) & (up_r < up_c + BLOCK)).astype(jnp.float32).astype(jnp.bfloat16)
    wide_r = lax.broadcasted_iota(jnp.int32, (blocks, tile), 0) * BLOCK
    wide_c = lax.broadcasted_iota(jnp.int32, (blocks, tile), 1)
    wide = ((wide_c >= wide_r) & (wide_c < wide_r + BLOCK)).astype(jnp.float32).astype(jnp.bfloat16)

    @pl.loop(0, 18)
    def _(i):
        c = i // 9
        o = i % 9
        pat = pattern[0, c, o].astype(jnp.float32).astype(jnp.bfloat16)
        part = jnp.dot(pat, wide, preferred_element_type=jnp.float32).astype(jnp.bfloat16)
        m = jnp.dot(up, part, preferred_element_type=jnp.float32)
        mask[c, o] = m.astype(jnp.bfloat16)
        q[1, 1 + c, o] = (base[0, c, o].astype(jnp.float32) * m).astype(jnp.bfloat16)

    pl.semaphore_wait(barrier, 8)

    halo = []
    for k, (dr, dc, c, first, count) in enumerate(HALO):
        copy = pltpu.make_async_remote_copy(
            src_ref=q.at[1, 1 + c, pl.ds(first, count)],
            dst_ref=q.at[1 - dr, 1 + c - 2 * dc, pl.ds(first, count)],
            send_sem=h_send.at[k],
            recv_sem=h_recv.at[k],
            device_id=device(dr, dc),
            device_id_type=MESH,
        )
        copy.start()
        halo.append(copy)

    @pl.loop(0, 18)
    def _(i):
        c = i // 9
        o = i % 9
        m = mask[c, o].astype(jnp.float32)
        p[c, o] = (tangent[0, c, o].astype(jnp.float32) * m).astype(jnp.bfloat16)

    def flip(node, o):
        sx, sy = shifts(o)
        nx, ny = node
        q[1 + nx + sx, 1 + ny + sy, 8 - o] = q[1 + nx, 1 + ny, o].T

    for c in range(2):
        for o in range(9):
            if not is_local(c, o):
                flip((0, c), o)

    for copy, (dr, dc, c, first, count) in zip(halo, HALO):
        copy.wait_recv()
        for o in range(first, first + count):
            if o != 4:
                flip((-dr, c - 2 * dc), o)

    def product(left, c, target):
        total = None
        for first, second in sources(target):
            ax, ay = shifts(first)
            term = jnp.dot(
                left[c, first], q[1 + ax, c + 1 + ay, second],
                preferred_element_type=jnp.float32,
            )
            total = term if total is None else total + term
        return total

    def returned(src, dst, send, recv, c, o):
        dr, dc, other = place(c, o)
        k = REMOTE.index((c, o))
        return pltpu.make_async_remote_copy(
            src_ref=src.at[c, o],
            dst_ref=dst.at[other, 8 - o],
            send_sem=send.at[k],
            recv_sem=recv.at[k],
            device_id=device(dr, dc),
            device_id_type=MESH,
        )

    def hand_over(src, dst, send, recv, o):
        for c in range(2):
            if is_local(c, o):
                dst[place(c, o)[2], 8 - o] = src[c, o]
            else:
                returned(src, dst, send, recv, c, o).start()

    for o in ORDER:
        @pl.loop(0, 2)
        def _(c):
            total = product(p, c, o) * mask[c, o].astype(jnp.float32)
            r32[c, o] = total
            half = total.astype(jnp.bfloat16)
            rb[c, o] = half
            rt[c, o] = half.T

        hand_over(rt, f, r_send, r_recv, o)

    for o in ORDER:
        @pl.loop(0, 2)
        def _(c):
            g[c, o] = product(rb, c, o).astype(jnp.bfloat16).T

        hand_over(g, gt, g_send, g_recv, o)

    for c, o in REMOTE:
        returned(rt, f, r_send, r_recv, c, o).wait_recv()

    @pl.loop(0, 18)
    def _(i):
        c = i // 9
        o = i % 9
        total = r32[c, o] + f[c, o].astype(jnp.float32)
        r32[c, o] = 3.0 * total
        s[c, o] = total.astype(jnp.bfloat16)

    for o in ORDER:
        @pl.loop(0, 2)
        def _(c):
            r32[c, o] = r32[c, o] - 2.0 * mask[c, o].astype(jnp.float32) * product(s, c, o)

    for c, o in REMOTE:
        returned(g, gt, g_send, g_recv, c, o).wait_recv()

    @pl.loop(0, 18)
    def _(i):
        c = i // 9
        o = i % 9
        m = mask[c, o].astype(jnp.float32)
        total = r32[c, o] - 2.0 * m * gt[c, o].astype(jnp.float32)
        out[0, c, o] = total.astype(jnp.bfloat16)

    for copy in halo:
        copy.wait_send()
    for c, o in REMOTE:
        returned(rt, f, r_send, r_recv, c, o).wait_send()
        returned(g, gt, g_send, g_recv, c, o).wait_send()


def shards(rows, cols, base_density, tangent_density, pattern):
    tile = base_density.shape[-1]
    tiles = (2, 9, tile, tile)
    vmem = pl.BlockSpec(memory_space=pltpu.VMEM)
    small = pltpu.VMEM(tiles, jnp.bfloat16)
    remote = len(REMOTE)
    return pl.pallas_call(
        functools.partial(kernel, rows, cols),
        out_shape=jax.ShapeDtypeStruct(base_density.shape, jnp.bfloat16),
        in_specs=[vmem] * 3,
        out_specs=vmem,
        scratch_shapes=[
            pltpu.VMEM((3, 4, 9, tile, tile), jnp.bfloat16),
            small,
            small,
            pltpu.VMEM(tiles, jnp.float32),
            small,
            small,
            small,
            small,
            small,
            small,
            pltpu.SemaphoreType.DMA((len(HALO),)),
            pltpu.SemaphoreType.DMA((len(HALO),)),
            pltpu.SemaphoreType.DMA((remote,)),
            pltpu.SemaphoreType.DMA((remote,)),
            pltpu.SemaphoreType.DMA((remote,)),
            pltpu.SemaphoreType.DMA((remote,)),
        ],
        compiler_params=pltpu.CompilerParams(
            collective_id=0, has_side_effects=True, vmem_limit_bytes=56 * 2**20
        ),
        name="tangent_step",
    )(base_density, tangent_density, pattern)


def solution(mesh):
    spec = P(("groups", "row"), "col", None, None, None)
    return jax.shard_map(
        functools.partial(shards, mesh.shape["row"], mesh.shape["col"]),
        mesh=mesh,
        in_specs=(spec, spec, P("row", "col", None, None, None)),
        out_specs=spec,
        check_vma=False,
    )
```

```python
import functools

import jax
import jax.numpy as jnp
from jax import lax
from jax.experimental import pallas as pl
from jax.experimental.pallas import tpu as pltpu
from jax.sharding import PartitionSpec as P

BLOCK = 23
MESH = pl.DeviceIdType.MESH
ORDER = (0, 1, 2, 6, 7, 8, 3, 5, 4)


def shifts(offset):
    return (offset // 3 - 1, offset % 3 - 1)


def sources(target):
    out = []
    for first in range(9):
        fx, fy = shifts(first)
        tx, ty = shifts(target)
        sx, sy = tx - fx, ty - fy
        if abs(sx) <= 1 and abs(sy) <= 1:
            out.append((first, (sx + 1) * 3 + sy + 1))
    return out


def side_plan():
    plan = [(1, 1, first, count) for first, count in ((1, 2), (4, 1), (7, 2))]
    plan += [(-1, 0, first, count) for first, count in ((0, 2), (4, 1), (6, 2))]
    return plan


PASS_ON = ((1, 1, 4, 2), (-1, 0, 4, 1))
LANES = 128
FOLD = 96


def place(col, offset):
    sx, sy = shifts(offset)
    y = col + sy
    return sx, y // 2, y % 2


def is_local(col, offset):
    sx, dc, _ = place(col, offset)
    return sx == 0 and dc == 0


SIDE = side_plan()
STEPS = (1, -1)
REMOTE = [(c, o) for o in ORDER for c in range(2) if not is_local(c, o)]


def fold(ref, value):
    tile = value.shape[-1]
    rest = tile - LANES
    ref[:, 0:rest] = value[0:FOLD, LANES:tile]
    ref[0 : tile - FOLD, LANES // 2 : LANES // 2 + rest] = value[FOLD:tile, LANES:tile]


def unfold(ref, folded):
    tile = ref.shape[-1]
    rest = tile - LANES
    ref[0:FOLD, LANES:tile] = folded[:, 0:rest]
    ref[FOLD:tile, LANES:tile] = folded[0 : tile - FOLD, LANES // 2 : LANES // 2 + rest]


def kernel(
    rows, cols, base, tangent, pattern, out,
    q, p, mask, r32, rb, rt, f, gt, g, s,
    own_fold, halo_fold, rt_fold, f_fold, g_fold, gt_fold,
    z_send, z_recv, h_send, h_recv, n_send, n_recv, r_send, r_recv, g_send, g_recv,
):
    group = lax.axis_index("groups")
    row = lax.axis_index("row")
    col = lax.axis_index("col")
    tile = base.shape[-1]

    def device(dr, dc):
        return (group, lax.rem(row + dr + rows, rows), lax.rem(col + dc + cols, cols))

    barrier = pltpu.get_barrier_semaphore()
    around = [(a, b) for a in (-1, 0, 1) for b in (-1, 0, 1) if (a, b) != (0, 0)]
    for dr, dc in around:
        pl.semaphore_signal(barrier, inc=1, device_id=device(dr, dc), device_id_type=MESH)

    blocks = pattern.shape[-1]
    up_r = lax.broadcasted_iota(jnp.int32, (tile, blocks), 0)
    up_c = lax.broadcasted_iota(jnp.int32, (tile, blocks), 1) * BLOCK
    up = ((up_r >= up_c) & (up_r < up_c + BLOCK)).astype(jnp.float32).astype(jnp.bfloat16)
    wide_r = lax.broadcasted_iota(jnp.int32, (blocks, tile), 0) * BLOCK
    wide_c = lax.broadcasted_iota(jnp.int32, (blocks, tile), 1)
    wide = ((wide_c >= wide_r) & (wide_c < wide_r + BLOCK)).astype(jnp.float32).astype(jnp.bfloat16)

    def prepare(c, o):
        pat = pattern[0, c, o].astype(jnp.float32).astype(jnp.bfloat16)
        part = jnp.dot(pat, wide, preferred_element_type=jnp.float32).astype(jnp.bfloat16)
        m = jnp.dot(up, part, preferred_element_type=jnp.float32)
        mask[c, o] = m.astype(jnp.bfloat16)
        kept = (base[0, c, o].astype(jnp.float32) * m).astype(jnp.bfloat16)
        q[1, 1 + c, o] = kept
        return kept

    @pl.loop(0, 2)
    def _(c):
        for e in range(2):
            fold(own_fold.at[c, e], prepare(c, 4 + e))

    pl.semaphore_wait(barrier, 8)

    def over_rows(k):
        left = (pl.ds(1, 2), pl.ds(4, 2), slice(None), pl.ds(0, LANES))
        return [
            pltpu.make_async_remote_copy(
                src_ref=q.at[(1,) + left],
                dst_ref=q.at[(1 - STEPS[k],) + left],
                send_sem=z_send.at[k, 0],
                recv_sem=z_recv.at[k, 0],
                device_id=device(STEPS[k], 0),
                device_id_type=MESH,
            ),
            pltpu.make_async_remote_copy(
                src_ref=own_fold,
                dst_ref=halo_fold.at[k],
                send_sem=z_send.at[k, 1],
                recv_sem=z_recv.at[k, 1],
                device_id=device(STEPS[k], 0),
                device_id_type=MESH,
            ),
        ]

    def within_row(x, dc, c, first, count, send, recv):
        return pltpu.make_async_remote_copy(
            src_ref=q.at[x, 1 + c, pl.ds(first, count)],
            dst_ref=q.at[x, 1 + c - 2 * dc, pl.ds(first, count)],
            send_sem=send,
            recv_sem=recv,
            device_id=device(0, dc),
            device_id_type=MESH,
        )

    halo = [over_rows(k) for k in range(2)]
    for pair in halo:
        for copy in pair:
            copy.start()

    @pl.loop(0, 2)
    def _(c):
        for o in (0, 1, 2, 3, 6, 7, 8):
            prepare(c, o)

    side = []
    for k, (dc, c, first, count) in enumerate(SIDE):
        copy = within_row(1, dc, c, first, count, h_send.at[k], h_recv.at[k])
        copy.start()
        side.append(copy)

    @pl.loop(0, 18)
    def _(i):
        c = i // 9
        o = i % 9
        m = mask[c, o].astype(jnp.float32)
        p[c, o] = (tangent[0, c, o].astype(jnp.float32) * m).astype(jnp.bfloat16)

    def flip(node, o):
        sx, sy = shifts(o)
        nx, ny = node
        q[1 + nx + sx, 1 + ny + sy, 8 - o] = q[1 + nx, 1 + ny, o].T

    for c in range(2):
        for o in range(9):
            if not is_local(c, o):
                flip((0, c), o)

    for copy, (dc, c, first, count) in zip(side, SIDE):
        copy.wait_recv()
        for o in range(first, first + count):
            if o != 4:
                flip((0, c - 2 * dc), o)

    def product(left, c, target, near=None):
        total = None
        for first, second in sources(target):
            ax, ay = shifts(first)
            if near is not None and near != (ax == 0 or shifts(target)[0] == 0):
                continue
            term = jnp.dot(
                left[c, first], q[1 + ax, c + 1 + ay, second],
                preferred_element_type=jnp.float32,
            )
            total = term if total is None else total + term
        return total

    def returned(src, dst, src_fold, dst_fold, send, recv, c, o):
        dr, dc, other = place(c, o)
        k = REMOTE.index((c, o))
        left = (slice(None), pl.ds(0, LANES))
        pairs = (
            (src.at[(c, o) + left], dst.at[(other, 8 - o) + left]),
            (src_fold.at[c, o], dst_fold.at[other, 8 - o]),
        )
        return [
            pltpu.make_async_remote_copy(
                src_ref=here,
                dst_ref=there,
                send_sem=send.at[k, i],
                recv_sem=recv.at[k, i],
                device_id=device(dr, dc),
                device_id_type=MESH,
            )
            for i, (here, there) in enumerate(pairs)
        ]

    back_r = functools.partial(returned, rt, f, rt_fold, f_fold, r_send, r_recv)
    back_g = functools.partial(returned, g, gt, g_fold, gt_fold, g_send, g_recv)

    def hand_over(back, src, dst, c, o):
        if is_local(c, o):
            dst[place(c, o)[2], 8 - o] = src[c, o]
        else:
            for copy in back(c, o):
                copy.start()

    def finish_r(c, o, total):
        total = total * mask[c, o].astype(jnp.float32)
        r32[c, o] = total
        half = total.astype(jnp.bfloat16)
        rb[c, o] = half
        turned = half.T
        rt[c, o] = turned
        fold(rt_fold.at[c, o], turned)

    for o in (3, 5, 4):
        @pl.loop(0, 2)
        def _(c):
            finish_r(c, o, product(p, c, o, True))

        for c in range(2):
            hand_over(back_r, rt, f, c, o)

    for o in (0, 1, 2, 6, 7, 8):
        @pl.loop(0, 2)
        def _(c):
            r32[c, o] = product(p, c, o, True)

    passed = []
    for k, dr in enumerate(STEPS):
        x = 1 - dr
        for copy in halo[k]:
            copy.wait_recv()
        for c in range(2):
            for e in range(2):
                unfold(q.at[x, 1 + c, 4 + e], halo_fold.at[k, c, e])
        for i, (dc, c, first, count) in enumerate(PASS_ON):
            copy = within_row(x, dc, c, first, count, n_send.at[k, i], n_recv.at[k, i])
            copy.start()
            passed.append(copy)
        flip((-dr, 0), 5)
        flip((-dr, 1), 5)
        for c, sy in ((1, 0), (1, -1), (0, 1)):
            o = (x * 3) + sy + 1
            finish_r(c, o, r32[c, o] + product(p, c, o, False))
            hand_over(back_r, rt, f, c, o)

    for copy in passed:
        copy.wait_recv()
    for dr in STEPS:
        x = 1 - dr
        flip((-dr, -1), 5)
        for c, sy in ((0, 0), (0, -1), (1, 1)):
            o = (x * 3) + sy + 1
            finish_r(c, o, r32[c, o] + product(p, c, o, False))
            hand_over(back_r, rt, f, c, o)

    for o in ORDER:
        @pl.loop(0, 2)
        def _(c):
            turned = product(rb, c, o).astype(jnp.bfloat16).T
            g[c, o] = turned
            fold(g_fold.at[c, o], turned)

        for c in range(2):
            hand_over(back_g, g, gt, c, o)

    for c, o in REMOTE:
        for copy in back_r(c, o):
            copy.wait_recv()
        other = place(c, o)[2]
        unfold(f.at[other, 8 - o], f_fold.at[other, 8 - o])

    @pl.loop(0, 18)
    def _(i):
        c = i // 9
        o = i % 9
        total = r32[c, o] + f[c, o].astype(jnp.float32)
        r32[c, o] = 3.0 * total
        s[c, o] = total.astype(jnp.bfloat16)

    for o in ORDER:
        @pl.loop(0, 2)
        def _(c):
            r32[c, o] = r32[c, o] - 2.0 * mask[c, o].astype(jnp.float32) * product(s, c, o)

    def finish(c, o):
        m = mask[c, o].astype(jnp.float32)
        total = r32[c, o] - 2.0 * m * gt[c, o].astype(jnp.float32)
        out[0, c, o] = total.astype(jnp.bfloat16)

    for o in ORDER:
        for c in range(2):
            if is_local(c, o):
                finish(place(c, o)[2], 8 - o)

    for c, o in REMOTE:
        other = place(c, o)[2]
        for copy in back_g(c, o):
            copy.wait_recv()
        unfold(gt.at[other, 8 - o], gt_fold.at[other, 8 - o])
        finish(other, 8 - o)

    for copy in halo[0] + halo[1] + side + passed:
        copy.wait_send()
    for c, o in REMOTE:
        for copy in back_r(c, o) + back_g(c, o):
            copy.wait_send()


def shards(rows, cols, base_density, tangent_density, pattern):
    tile = base_density.shape[-1]
    tiles = (2, 9, tile, tile)
    vmem = pl.BlockSpec(memory_space=pltpu.VMEM)
    small = pltpu.VMEM(tiles, jnp.bfloat16)
    folded = pltpu.VMEM((2, 9, FOLD, LANES), jnp.bfloat16)
    dma = pltpu.SemaphoreType.DMA
    remote = len(REMOTE)
    return pl.pallas_call(
        functools.partial(kernel, rows, cols),
        out_shape=jax.ShapeDtypeStruct(base_density.shape, jnp.bfloat16),
        in_specs=[vmem] * 3,
        out_specs=vmem,
        scratch_shapes=[
            pltpu.VMEM((3, 4, 9, tile, tile), jnp.bfloat16),
            small,
            small,
            pltpu.VMEM(tiles, jnp.float32),
            small,
            small,
            small,
            small,
            small,
            small,
            pltpu.VMEM((2, 2, FOLD, LANES), jnp.bfloat16),
            pltpu.VMEM((2, 2, 2, FOLD, LANES), jnp.bfloat16),
            folded,
            folded,
            folded,
            folded,
            dma((2, 2)),
            dma((2, 2)),
            dma((len(SIDE),)),
            dma((len(SIDE),)),
            dma((2, len(PASS_ON))),
            dma((2, len(PASS_ON))),
            dma((remote, 2)),
            dma((remote, 2)),
            dma((remote, 2)),
            dma((remote, 2)),
        ],
        compiler_params=pltpu.CompilerParams(
            collective_id=0, has_side_effects=True, vmem_limit_bytes=56 * 2**20
        ),
        name="tangent_step",
    )(base_density, tangent_density, pattern)


def solution(mesh):
    spec = P(("groups", "row"), "col", None, None, None)
    return jax.shard_map(
        functools.partial(shards, mesh.shape["row"], mesh.shape["col"]),
        mesh=mesh,
        in_specs=(spec, spec, P("row", "col", None, None, None)),
        out_specs=spec,
        check_vma=False,
    )
```

```python
import functools

import jax
import jax.numpy as jnp
from jax import lax
from jax.experimental import pallas as pl
from jax.experimental.pallas import tpu as pltpu
from jax.sharding import PartitionSpec as P

BLOCK = 23
MESH = pl.DeviceIdType.MESH
ORDER = (0, 1, 2, 6, 7, 8, 3, 5, 4)


def shifts(offset):
    return (offset // 3 - 1, offset % 3 - 1)


def sources(target):
    out = []
    for first in range(9):
        fx, fy = shifts(first)
        tx, ty = shifts(target)
        sx, sy = tx - fx, ty - fy
        if abs(sx) <= 1 and abs(sy) <= 1:
            out.append((first, (sx + 1) * 3 + sy + 1))
    return out


def side_plan():
    plan = [(1, 1, first, count) for first, count in ((1, 2), (4, 1), (7, 2))]
    plan += [(-1, 0, first, count) for first, count in ((0, 2), (4, 1), (6, 2))]
    return plan


PASS_ON = ((-1, 0, 4, 1), (1, 1, 4, 2))
LANES = 128
FOLD = 96


def place(col, offset):
    sx, sy = shifts(offset)
    y = col + sy
    return sx, y // 2, y % 2


def is_local(col, offset):
    sx, dc, _ = place(col, offset)
    return sx == 0 and dc == 0


SIDE = side_plan()
STEPS = (1, -1)
REMOTE = [(c, o) for o in ORDER for c in range(2) if not is_local(c, o)]


def fold(ref, value):
    tile = value.shape[-1]
    rest = tile - LANES
    ref[:, 0:rest] = value[0:FOLD, LANES:tile]
    ref[0 : tile - FOLD, LANES // 2 : LANES // 2 + rest] = value[FOLD:tile, LANES:tile]


def unfold(ref, folded):
    tile = ref.shape[-1]
    rest = tile - LANES
    ref[0:FOLD, LANES:tile] = folded[:, 0:rest]
    ref[FOLD:tile, LANES:tile] = folded[0 : tile - FOLD, LANES // 2 : LANES // 2 + rest]


def kernel(
    rows, cols, base_far, tangent_far, pattern_far, out,
    base, tangent, pattern, load,
    q, p, mask, r32, rb, rt, f, gt, g, s,
    own_fold, halo_fold, rt_fold, f_fold, g_fold, gt_fold,
    z_send, z_recv, h_send, h_recv, n_send, n_recv, r_send, r_recv, g_send, g_recv,
):
    group = lax.axis_index("groups")
    row = lax.axis_index("row")
    col = lax.axis_index("col")
    tile = base.shape[-1]

    loads = [
        pltpu.make_async_copy(far, near, load.at[k])
        for k, (far, near) in enumerate(
            ((pattern_far, pattern), (base_far, base), (tangent_far, tangent))
        )
    ]
    for copy in loads:
        copy.start()

    def device(dr, dc):
        return (group, lax.rem(row + dr + rows, rows), lax.rem(col + dc + cols, cols))

    barrier = pltpu.get_barrier_semaphore()
    around = [(a, b) for a in (-1, 0, 1) for b in (-1, 0, 1) if (a, b) != (0, 0)]
    for dr, dc in around:
        pl.semaphore_signal(barrier, inc=1, device_id=device(dr, dc), device_id_type=MESH)

    blocks = pattern.shape[-1]
    up_r = lax.broadcasted_iota(jnp.int32, (tile, blocks), 0)
    up_c = lax.broadcasted_iota(jnp.int32, (tile, blocks), 1) * BLOCK
    up = ((up_r >= up_c) & (up_r < up_c + BLOCK)).astype(jnp.float32).astype(jnp.bfloat16)
    wide_r = lax.broadcasted_iota(jnp.int32, (blocks, tile), 0) * BLOCK
    wide_c = lax.broadcasted_iota(jnp.int32, (blocks, tile), 1)
    wide = ((wide_c >= wide_r) & (wide_c < wide_r + BLOCK)).astype(jnp.float32).astype(jnp.bfloat16)

    loads[0].wait()
    loads[1].wait()

    def prepare(c, o):
        pat = pattern[0, c, o].astype(jnp.float32).astype(jnp.bfloat16)
        part = jnp.dot(pat, wide, preferred_element_type=jnp.float32).astype(jnp.bfloat16)
        m = jnp.dot(up, part, preferred_element_type=jnp.float32)
        mask[c, o] = m.astype(jnp.bfloat16)
        kept = (base[0, c, o].astype(jnp.float32) * m).astype(jnp.bfloat16)
        q[1, 1 + c, o] = kept
        return kept

    def over_rows(k, c):
        left = (1 + c, pl.ds(4, 2), slice(None), pl.ds(0, LANES))
        return [
            pltpu.make_async_remote_copy(
                src_ref=q.at[(1,) + left],
                dst_ref=q.at[(1 - STEPS[k],) + left],
                send_sem=z_send.at[k, c, 0],
                recv_sem=z_recv.at[k, c, 0],
                device_id=device(STEPS[k], 0),
                device_id_type=MESH,
            ),
            pltpu.make_async_remote_copy(
                src_ref=own_fold.at[c],
                dst_ref=halo_fold.at[k, c],
                send_sem=z_send.at[k, c, 1],
                recv_sem=z_recv.at[k, c, 1],
                device_id=device(STEPS[k], 0),
                device_id_type=MESH,
            ),
        ]

    def within_row(x, dc, c, first, count, send, recv):
        return pltpu.make_async_remote_copy(
            src_ref=q.at[x, 1 + c, pl.ds(first, count)],
            dst_ref=q.at[x, 1 + c - 2 * dc, pl.ds(first, count)],
            send_sem=send,
            recv_sem=recv,
            device_id=device(0, dc),
            device_id_type=MESH,
        )

    halo = [[over_rows(k, c) for c in range(2)] for k in range(2)]
    for c in range(2):
        for e in range(2):
            fold(own_fold.at[c, e], prepare(c, 4 + e))
        if c == 0:
            pl.semaphore_wait(barrier, 8)
        for k in range(2):
            for copy in halo[k][c]:
                copy.start()

    @pl.loop(0, 2)
    def _(c):
        for o in (0, 1, 2, 3, 6, 7, 8):
            prepare(c, o)

    side = []
    for k, (dc, c, first, count) in enumerate(SIDE):
        copy = within_row(1, dc, c, first, count, h_send.at[k], h_recv.at[k])
        copy.start()
        side.append(copy)

    loads[2].wait()

    @pl.loop(0, 18)
    def _(i):
        c = i // 9
        o = i % 9
        m = mask[c, o].astype(jnp.float32)
        p[c, o] = (tangent[0, c, o].astype(jnp.float32) * m).astype(jnp.bfloat16)

    def flip(node, o):
        sx, sy = shifts(o)
        nx, ny = node
        q[1 + nx + sx, 1 + ny + sy, 8 - o] = q[1 + nx, 1 + ny, o].T

    for c in range(2):
        for o in range(9):
            if not is_local(c, o):
                flip((0, c), o)

    for copy, (dc, c, first, count) in zip(side, SIDE):
        copy.wait_recv()
        for o in range(first, first + count):
            if o != 4:
                flip((0, c - 2 * dc), o)

    def product(left, c, target, near=None):
        total = None
        for first, second in sources(target):
            ax, ay = shifts(first)
            if near is not None and near != (ax == 0 or shifts(target)[0] == 0):
                continue
            term = jnp.dot(
                left[c, first], q[1 + ax, c + 1 + ay, second],
                preferred_element_type=jnp.float32,
            )
            total = term if total is None else total + term
        return total

    def returned(src, dst, src_fold, dst_fold, send, recv, c, o):
        dr, dc, other = place(c, o)
        k = REMOTE.index((c, o))
        left = (slice(None), pl.ds(0, LANES))
        pairs = (
            (src.at[(c, o) + left], dst.at[(other, 8 - o) + left]),
            (src_fold.at[c, o], dst_fold.at[other, 8 - o]),
        )
        return [
            pltpu.make_async_remote_copy(
                src_ref=here,
                dst_ref=there,
                send_sem=send.at[k, i],
                recv_sem=recv.at[k, i],
                device_id=device(dr, dc),
                device_id_type=MESH,
            )
            for i, (here, there) in enumerate(pairs)
        ]

    back_r = functools.partial(returned, rt, f, rt_fold, f_fold, r_send, r_recv)
    back_g = functools.partial(returned, g, gt, g_fold, gt_fold, g_send, g_recv)

    def hand_over(back, src, dst, c, o):
        if is_local(c, o):
            dst[place(c, o)[2], 8 - o] = src[c, o]
        else:
            for copy in back(c, o):
                copy.start()

    def finish_r(c, o, total):
        total = total * mask[c, o].astype(jnp.float32)
        r32[c, o] = total
        half = total.astype(jnp.bfloat16)
        rb[c, o] = half
        turned = half.T
        rt[c, o] = turned
        fold(rt_fold.at[c, o], turned)

    for o in (3, 5, 4):
        @pl.loop(0, 2)
        def _(c):
            finish_r(c, o, product(p, c, o, True))

        for c in range(2):
            hand_over(back_r, rt, f, c, o)

    for o in (0, 1, 2, 6, 7, 8):
        @pl.loop(0, 2)
        def _(c):
            r32[c, o] = product(p, c, o, True)

    def complete(c, o):
        finish_r(c, o, r32[c, o] + product(p, c, o, False))
        hand_over(back_r, rt, f, c, o)

    passed = []
    for c in range(2):
        for k, dr in enumerate(STEPS):
            x = 1 - dr
            for copy in halo[k][c]:
                copy.wait_recv()
            for e in range(2):
                unfold(q.at[x, 1 + c, 4 + e], halo_fold.at[k, c, e])
            dc, _, first, count = PASS_ON[c]
            copy = within_row(x, dc, c, first, count, n_send.at[k, c], n_recv.at[k, c])
            copy.start()
            passed.append(copy)
            flip((-dr, c), 5)
            for own, sy in (((1, -1),), ((1, 0), (0, 1)))[c]:
                complete(own, x * 3 + sy + 1)

    for copy in passed:
        copy.wait_recv()
    for dr in STEPS:
        x = 1 - dr
        flip((-dr, -1), 5)
        for c, sy in ((0, 0), (0, -1), (1, 1)):
            complete(c, x * 3 + sy + 1)

    for o in ORDER:
        @pl.loop(0, 2)
        def _(c):
            turned = product(rb, c, o).astype(jnp.bfloat16).T
            g[c, o] = turned
            fold(g_fold.at[c, o], turned)

        for c in range(2):
            hand_over(back_g, g, gt, c, o)

    for c, o in REMOTE:
        for copy in back_r(c, o):
            copy.wait_recv()
        other = place(c, o)[2]
        unfold(f.at[other, 8 - o], f_fold.at[other, 8 - o])

    @pl.loop(0, 18)
    def _(i):
        c = i // 9
        o = i % 9
        total = r32[c, o] + f[c, o].astype(jnp.float32)
        r32[c, o] = 3.0 * total
        s[c, o] = total.astype(jnp.bfloat16)

    for o in ORDER:
        @pl.loop(0, 2)
        def _(c):
            r32[c, o] = r32[c, o] - 2.0 * mask[c, o].astype(jnp.float32) * product(s, c, o)

    def finish(c, o):
        m = mask[c, o].astype(jnp.float32)
        total = r32[c, o] - 2.0 * m * gt[c, o].astype(jnp.float32)
        out[0, c, o] = total.astype(jnp.bfloat16)

    for o in ORDER:
        for c in range(2):
            if is_local(c, o):
                finish(place(c, o)[2], 8 - o)

    for c, o in REMOTE:
        other = place(c, o)[2]
        for copy in back_g(c, o):
            copy.wait_recv()
        unfold(gt.at[other, 8 - o], gt_fold.at[other, 8 - o])
        finish(other, 8 - o)

    for copy in sum(halo[0] + halo[1], []) + side + passed:
        copy.wait_send()
    for c, o in REMOTE:
        for copy in back_r(c, o) + back_g(c, o):
            copy.wait_send()


def shards(rows, cols, base_density, tangent_density, pattern):
    tile = base_density.shape[-1]
    tiles = (2, 9, tile, tile)
    vmem = pl.BlockSpec(memory_space=pltpu.VMEM)
    small = pltpu.VMEM(tiles, jnp.bfloat16)
    folded = pltpu.VMEM((2, 9, FOLD, LANES), jnp.bfloat16)
    dma = pltpu.SemaphoreType.DMA
    remote = len(REMOTE)
    return pl.pallas_call(
        functools.partial(kernel, rows, cols),
        out_shape=jax.ShapeDtypeStruct(base_density.shape, jnp.bfloat16),
        in_specs=[pl.BlockSpec(memory_space=pl.ANY)] * 3,
        out_specs=vmem,
        scratch_shapes=[
            pltpu.VMEM(base_density.shape, jnp.bfloat16),
            pltpu.VMEM(base_density.shape, jnp.bfloat16),
            pltpu.VMEM(pattern.shape, pattern.dtype),
            dma((3,)),
            pltpu.VMEM((3, 4, 9, tile, tile), jnp.bfloat16),
            small,
            small,
            pltpu.VMEM(tiles, jnp.float32),
            small,
            small,
            small,
            small,
            small,
            small,
            pltpu.VMEM((2, 2, FOLD, LANES), jnp.bfloat16),
            pltpu.VMEM((2, 2, 2, FOLD, LANES), jnp.bfloat16),
            folded,
            folded,
            folded,
            folded,
            dma((2, 2, 2)),
            dma((2, 2, 2)),
            dma((len(SIDE),)),
            dma((len(SIDE),)),
            dma((2, len(PASS_ON))),
            dma((2, len(PASS_ON))),
            dma((remote, 2)),
            dma((remote, 2)),
            dma((remote, 2)),
            dma((remote, 2)),
        ],
        compiler_params=pltpu.CompilerParams(
            collective_id=0, has_side_effects=True, vmem_limit_bytes=56 * 2**20
        ),
        name="tangent_step",
    )(base_density, tangent_density, pattern)


def solution(mesh):
    spec = P(("groups", "row"), "col", None, None, None)
    return jax.shard_map(
        functools.partial(shards, mesh.shape["row"], mesh.shape["col"]),
        mesh=mesh,
        in_specs=(spec, spec, P("row", "col", None, None, None)),
        out_specs=spec,
        check_vma=False,
    )
```
